32 devices in a mesh: rep: 4 (over x, core), shard: 8 (over z, y).
Axes of the slice: x: 2, y: 2, z: 4, core: 2. Of those that a mesh axis runs over, the one named last changes fastest.
Arguments:
- tokens: bfloat16 [8, 2048, 896], P('rep', 'shard'), may hold values from -6 to 6
- segments: int32 [8, 2048], P('rep', 'shard'), may hold values from 0 to 2, as said below
- first_gain: bfloat16 [896], P('shard'), may hold values from 0.5 to 1.5
- query_weight: bfloat16 [896, 896], P('shard'), may hold values from -0.1875 to 0.1875
- query_bias: bfloat16 [896], P('shard'), may hold values from -3 to 3
- key_weight: bfloat16 [896, 128], P('shard'), may hold values from -0.1875 to 0.1875
- key_bias: bfloat16 [128], P('shard'), may hold values from -3 to 3
- value_weight: bfloat16 [896, 128], P('shard'), may hold values from -0.1875 to 0.1875
- value_bias: bfloat16 [128], P('shard'), may hold values from -3 to 3
- out_weight: bfloat16 [896, 896], P('shard'), may hold values from -0.75 to 0.75
- second_gain: bfloat16 [896], P('shard'), may hold values from 0.5 to 1.5
- gate_weight: bfloat16 [896, 4864], P('shard'), may hold values from -0.1875 to 0.1875
- up_weight: bfloat16 [896, 4864], P('shard'), may hold values from -0.1875 to 0.1875
- down_weight: bfloat16 [4864, 896], P('shard'), may hold values from -0.125 to 0.125
- cotangent: bfloat16 [8, 2048, 896], P('rep', 'shard'), may hold values from -6 to 6
Outputs:
- output: bfloat16 [8, 2048, 896], P('rep', 'shard')
- tokens_grad: bfloat16 [8, 2048, 896], P('rep', 'shard')
- first_gain_grad: float32 [896], P('shard')
- query_weight_grad: float32 [896, 896], P('shard')
- query_bias_grad: float32 [896], P('shard')
- key_weight_grad: float32 [896, 128], P('shard')
- key_bias_grad: float32 [128], P('shard')
- value_weight_grad: float32 [896, 128], P('shard')
- value_bias_grad: float32 [128], P('shard')
- out_weight_grad: float32 [896, 896], P('shard')
- second_gain_grad: float32 [896], P('shard')
- gate_weight_grad: float32 [896, 4864], P('shard')
- up_weight_grad: float32 [896, 4864], P('shard')
- down_weight_grad: float32 [4864, 896], P('shard')
The draws below stay inside these ranges and needn't reach their ends.
Inputs may be any that keep to these rules, and one draw needn't show every extreme that they name: `segments`: along each sequence the segment numbers start at 0 and never fall.
All inputs are finite; a program needn't handle non-finite values.
Results may differ from the reference program's by a relative error of at most 0.033.
Values may be sent and summed in bfloat16 or wider, within the bound.
A program may use at most 320 MiB of HBM per device.

```python
import jax
import jax.numpy as jnp
from jax import lax

D = 896
HD = 64
FF = 4864
QD = 896
KD = 128
SEQ_LEN = 2048
SEQS = 2
SEQUENCES = 8
N_REP = 4


def draw_segments(key, part):
    subkeys = jax.random.split(key, 4)
    columns = jnp.arange(SEQ_LEN, dtype=jnp.int32)[None, :]
    ticket = jax.random.randint(subkeys[0], (SEQUENCES, SEQ_LEN), 0, max(SEQ_LEN // 4, 2))
    random_starts = (ticket == 0) & (columns > 0)
    chosen = jax.random.randint(subkeys[1], (N_REP,), 0, SEQS)
    border = max(SEQ_LEN // 8, 2)
    first_cut = jax.random.randint(subkeys[2], (N_REP,), 1, border)
    last_cut = jax.random.randint(subkeys[3], (N_REP,), SEQ_LEN - border + 1, SEQ_LEN)
    row_index = jnp.arange(SEQUENCES, dtype=jnp.int32)
    group_of = row_index // SEQS
    picked = row_index - group_of * SEQS == chosen[group_of]
    fixed_starts = (columns == first_cut[group_of][:, None]) | (columns == last_cut[group_of][:, None])
    starts = jnp.where(picked[:, None], fixed_starts, random_starts)
    numbers = jnp.cumsum(starts.astype(jnp.int32), axis=1)
    return jnp.minimum(numbers, 2).astype(jnp.int32)


def levels(own_key, shape, cuts, low, largest):
    level, own = 1.0, jax.random.fold_in(own_key, 6)
    for dim, blocks in cuts:
        draws = jnp.exp(jax.random.uniform(jax.random.fold_in(own, dim), (blocks,), jnp.float32, low / len(cuts), largest / len(cuts)))
        level = level * jnp.repeat(draws, shape[dim] // blocks).reshape([-1 if axis == dim else 1 for axis in range(len(shape))])
    return level


def bell_draw(rng, shape, scale, most, shards=(), kind=jnp.bfloat16):
    loudness = levels(rng, shape, shards, -0.22, 0.18) if shards else 1.0
    entries = jax.random.normal(rng, shape, jnp.float32) * scale * loudness
    return jnp.minimum(jnp.maximum(entries, -most), most).astype(kind)


def setup_inputs(seed: int = 0) -> dict:
    splits = jax.random.split(jax.random.key(seed), 16)
    return {
        "tokens": bell_draw(splits[0], (SEQUENCES, SEQ_LEN, D), 1.0, 6.0, ((0, 4), (1, 8))),
        "segments": draw_segments(jax.random.fold_in(splits[15], 71), 0),
        "first_gain": jnp.clip(1.0 + 0.1 * jax.random.normal(splits[2], (D,), jnp.float32), 0.5, 1.5).astype(jnp.bfloat16),
        "query_weight": bell_draw(splits[3], (D, QD), D ** -0.5, 0.1875, ((0, 8),)),
        "query_bias": bell_draw(splits[4], (QD,), 0.5, 3.0, ((0, 8),)),
        "key_weight": bell_draw(splits[5], (D, KD), D ** -0.5, 0.1875, ((0, 8),)),
        "key_bias": bell_draw(splits[6], (KD,), 0.5, 3.0, ((0, 8),)),
        "value_weight": bell_draw(splits[7], (D, KD), D ** -0.5, 0.1875, ((0, 8),)),
        "value_bias": bell_draw(splits[8], (KD,), 0.5, 3.0, ((0, 8),)),
        "out_weight": bell_draw(splits[9], (QD, D), (QD // 16) ** -0.5, 0.75, ((0, 8),)),
        "second_gain": jnp.clip(1.0 + 0.1 * jax.random.normal(splits[10], (D,), jnp.float32), 0.5, 1.5).astype(jnp.bfloat16),
        "gate_weight": bell_draw(splits[11], (D, FF), D ** -0.5, 0.1875, ((0, 8),)),
        "up_weight": bell_draw(splits[12], (D, FF), D ** -0.5, 0.1875, ((0, 8),)),
        "down_weight": bell_draw(splits[13], (FF, D), (FF // 2) ** -0.5, 0.125, ((0, 8),)),
        "cotangent": bell_draw(splits[14], (SEQUENCES, SEQ_LEN, D), 1.0, 6.0, ((0, 4), (1, 8))),
    }


@jax.custom_vjp
def low(v):
    return lax.optimization_barrier(v.astype(jnp.bfloat16)).astype(jnp.float32)

@jax.custom_vjp
def low_back(v):
    return v

def low_keep(v):
    return (low(v), None)

def low_pass(kept, grad):
    return (grad,)

def back_keep(v):
    return (v, None)

def back_low(kept, grad):
    return (low(grad),)
low.defvjp(low_keep, low_pass)
low_back.defvjp(back_keep, back_low)
EXACT = lax.Precision.HIGHEST
EPSILON = 1e-06
THETA = 1000000.0
MASKED = -1000000000.0

def product(left_side, right_side):
    return jnp.dot(left_side, right_side, precision=EXACT)

def rms_scale(values):
    return lax.rsqrt(lax.optimization_barrier(jnp.mean(values * values, axis=-1, keepdims=True)) + EPSILON)

def rotate(values, cosine, sine_table):
    half_size = values.shape[-1] // 2
    first_half = values[..., :half_size]
    second_half = values[..., half_size:]
    cosine = cosine[:, None, :]
    sine_table = sine_table[:, None, :]
    return jnp.concatenate([first_half * cosine - second_half * sine_table, second_half * cosine + first_half * sine_table], axis=-1)

def layer_forward(inputs, segment, weight_set):
    gain_first, query_matrix, query_vector, key_matrix, key_vector, value_matrix, value_vector, output_matrix, gain_second, gate_matrix, up_matrix, down_matrix = weight_set
    token_count = inputs.shape[0]
    head_count = query_matrix.shape[1] // HD
    shared_heads = key_matrix.shape[1] // HD
    group_size = head_count // shared_heads
    places = jnp.arange(token_count, dtype=jnp.int32)
    earlier = lax.optimization_barrier(jnp.sum((segment[None, :] < segment[:, None]).astype(jnp.int32), axis=1))
    position = places - earlier
    frequency = jnp.power(THETA, -(jnp.arange(HD // 2, dtype=jnp.float32) * 2.0 / HD))
    angles = position.astype(jnp.float32)[:, None] * frequency[None, :]
    cosine = jnp.cos(angles)
    sine_table = jnp.sin(angles)
    normed_first = low(inputs * rms_scale(inputs) * gain_first)
    query_linear = low_back(product(normed_first, query_matrix) + query_vector)
    key_linear = low_back(product(normed_first, key_matrix) + key_vector)
    values_all = low(low_back(product(normed_first, value_matrix) + value_vector))
    queries = low(rotate(query_linear.reshape(token_count, head_count, HD), cosine, sine_table))
    keys_all = low(rotate(key_linear.reshape(token_count, shared_heads, HD), cosine, sine_table))
    queries = queries.reshape(token_count, shared_heads, group_size, HD)
    values_heads = values_all.reshape(token_count, shared_heads, HD)
    scores = jnp.einsum('qkgd,skd->kgqs', queries, keys_all, precision=EXACT) * HD ** (-0.5)
    allowed = (segment[:, None] == segment[None, :]) & (places[:, None] >= places[None, :])
    scores = low_back(jnp.where(allowed, scores, MASKED))
    row_max = lax.optimization_barrier(jnp.max(scores, axis=-1, keepdims=True))
    weights = jnp.exp(scores - row_max)
    probs = low(weights / lax.optimization_barrier(jnp.sum(weights, axis=-1, keepdims=True)))
    mixed_heads = jnp.einsum('kgqs,skd->qkgd', probs, values_heads, precision=EXACT)
    mixed_heads = low(low_back(mixed_heads.reshape(token_count, head_count * HD)))
    hidden = inputs + low_back(product(mixed_heads, output_matrix))
    normed_second = low(hidden * rms_scale(hidden) * gain_second)
    gate_linear = low_back(product(normed_second, gate_matrix))
    up_linear = low_back(product(normed_second, up_matrix))
    activation = low(gate_linear * jax.nn.sigmoid(gate_linear) * up_linear)
    return hidden + low_back(product(activation, down_matrix))

def reference(tokens, segments, first_gain, query_weight, query_bias, key_weight, key_bias, value_weight, value_bias, out_weight, second_gain, gate_weight, up_weight, down_weight, cotangent):
    weight_set = tuple((weight.astype(jnp.float32) for weight in (first_gain, query_weight, query_bias, key_weight, key_bias, value_weight, value_bias, out_weight, second_gain, gate_weight, up_weight, down_weight)))

    def one_sequence(totals, element):
        inputs, segment, grad_output = element

        def forward(values, weight_list):
            return layer_forward(values, segment, weight_list)
        result, pullback = jax.vjp(forward, inputs.astype(jnp.float32), weight_set)
        grad_inputs, grad_weights = pullback(grad_output.astype(jnp.float32))
        totals = jax.tree.map(jnp.add, totals, grad_weights)
        return (totals, (result.astype(jnp.bfloat16), grad_inputs.astype(jnp.bfloat16)))
    starting = tuple((jnp.zeros_like(weight) for weight in weight_set))
    totals, (outputs, grads_inputs) = lax.scan(one_sequence, starting, (tokens, segments, cotangent))
    return (outputs, grads_inputs, totals[0], totals[1], totals[2], totals[3], totals[4], totals[5], totals[6], totals[7], totals[8], totals[9], totals[10], totals[11])
```

```python
import functools
import math

import jax
import jax.numpy as jnp
from jax import lax
from jax.sharding import PartitionSpec as P

HD = 64


EPSILON = 1e-06
THETA = 1000000.0
MASKED = -1000000000.0


def rms_scale(values):
    return lax.rsqrt(jnp.mean(values * values, axis=-1, keepdims=True) + EPSILON)


def rotate(values, cosine, sine_table):
    half_size = values.shape[-1] // 2
    first_half = values[..., :half_size]
    second_half = values[..., half_size:]
    cosine = cosine[:, None, :]
    sine_table = sine_table[:, None, :]
    return jnp.concatenate(
        [
            first_half * cosine - second_half * sine_table,
            second_half * cosine + first_half * sine_table,
        ],
        axis=-1,
    )


def inner_rows(left_side, right_side):
    return lax.dot_general(
        left_side, right_side, (((0,), (0,)), ((), ())), preferred_element_type=jnp.float32
    )


def times_transposed(left_side, right_side):
    return lax.dot_general(
        left_side, right_side, (((1,), (1,)), ((), ())), preferred_element_type=jnp.float32
    )


def norm_back(grad_normed, values, scale_rows, gain_value):
    normal = values * scale_rows
    grad_scaled = grad_normed * gain_value.astype(jnp.float32)
    return scale_rows * (
        grad_scaled - normal * jnp.mean(grad_scaled * normal, axis=-1, keepdims=True)
    )


def masked_scores(query_block, key_block, mask_block):
    raw_scores = jnp.einsum(
        "bqkgd,bskd->bkgqs", query_block, key_block, preferred_element_type=jnp.float32
    ) * HD ** (-0.5)
    return jnp.where(mask_block[:, None, None], raw_scores, MASKED)


def attend(items):
    query_block, key_block, value_block, mask_block = items
    scores = masked_scores(query_block, key_block, mask_block)
    row_max = jnp.max(scores, axis=-1, keepdims=True)
    weights = jnp.exp(scores - row_max)
    row_total = jnp.sum(weights, axis=-1, keepdims=True)
    probs = (weights / row_total).astype(jnp.bfloat16)
    mixed = jnp.einsum("bkgqs,bskd->bqkgd", probs, value_block, preferred_element_type=jnp.float32)
    return (mixed.astype(jnp.bfloat16), row_max + jnp.log(row_total))


def attend_back(items):
    query_block, key_block, value_block, mask_block, log_block, grad_block = items
    scores = masked_scores(query_block, key_block, mask_block)
    probs_full = jnp.exp(scores - log_block)
    grad_probs = jnp.einsum(
        "bqkgd,bskd->bkgqs", grad_block, value_block, preferred_element_type=jnp.float32
    )
    row_delta = jnp.sum(probs_full * grad_probs, axis=-1, keepdims=True)
    grad_scores = (probs_full * (grad_probs - row_delta)).astype(jnp.bfloat16)
    grad_query = jnp.einsum(
        "bkgqs,bskd->bqkgd", grad_scores, key_block, preferred_element_type=jnp.float32
    ) * HD ** (-0.5)
    grad_key = jnp.einsum(
        "bkgqs,bqkgd->bskd", grad_scores, query_block, preferred_element_type=jnp.float32
    ) * HD ** (-0.5)
    grad_value = jnp.einsum(
        "bkgqs,bqkgd->bskd",
        probs_full.astype(jnp.bfloat16),
        grad_block,
        preferred_element_type=jnp.float32,
    )
    return (grad_query, grad_key, grad_value)


def pack_rows(pieces, width):
    flat = jnp.concatenate(pieces)
    rows = -(-flat.shape[0] // (8 * width)) * 8
    return jnp.pad(flat, (0, rows * width - flat.shape[0])).reshape(rows, width)


def on_device(
    tokens,
    segments,
    first_gain,
    query_weight,
    query_bias,
    key_weight,
    key_bias,
    value_weight,
    value_bias,
    out_weight,
    second_gain,
    gate_weight,
    up_weight,
    down_weight,
    cotangent,
    reps,
    shards,
):
    sequences, local_tokens, model_width = tokens.shape
    row_count = sequences * local_tokens
    own_rows = first_gain.shape[0]
    query_width = query_weight.shape[1]
    key_width = key_weight.shape[1]
    hidden_width = gate_weight.shape[1]
    own_hidden = down_weight.shape[0]
    part_hidden = own_hidden // reps
    slice_width = part_hidden * shards
    padded_width = -(-slice_width // 128) * 128
    qkv_width = query_width + 2 * key_width
    head_count = query_width // HD
    shared_heads = key_width // HD
    group_size = head_count // shared_heads
    block_seqs = math.gcd(sequences, max(1, 512 // local_tokens))
    block_count = sequences // block_seqs
    rep_index = lax.axis_index("rep")

    def split(values):
        return values.reshape((block_count, block_seqs) + values.shape[1:])

    def pick_columns(weight):
        grouped = weight.reshape(own_rows, shards, reps, part_hidden)
        picked = lax.dynamic_index_in_dim(grouped, rep_index, 2, keepdims=False)
        return picked.reshape(own_rows, slice_width)

    def widen(values):
        return jnp.pad(values, ((0, 0), (0, padded_width - slice_width)))

    small = pack_rows(
        [
            first_gain,
            second_gain,
            query_bias,
            key_bias,
            value_bias,
            segments.reshape(-1).astype(jnp.bfloat16),
        ],
        qkv_width,
    )
    qkv_part = jnp.concatenate([query_weight, key_weight, value_weight], axis=1)
    first_set = lax.all_gather(
        jnp.concatenate([qkv_part, small], axis=0), "shard", axis=0, tiled=False
    )
    qkv_matrix = first_set[:, :own_rows].reshape(model_width, qkv_width)
    small_set = first_set[:, own_rows:].reshape(shards, -1)
    sizes = [own_rows, own_rows, own_rows, key_bias.shape[0], value_bias.shape[0]]
    starts = [sum(sizes[:i]) for i in range(len(sizes) + 1)]
    gain_first, gain_second, query_vector, key_vector, value_vector = [
        small_set[:, starts[i] : starts[i] + sizes[i]].reshape(-1) for i in range(len(sizes))
    ]
    qkv_vector = jnp.concatenate([query_vector, key_vector, value_vector])
    all_segments = (
        small_set[:, starts[-1] : starts[-1] + row_count]
        .reshape(shards, sequences, local_tokens)
        .transpose(1, 0, 2)
        .reshape(sequences, shards * local_tokens)
        .astype(jnp.int32)
    )
    full_length = all_segments.shape[1]
    offset = lax.axis_index("shard") * local_tokens
    places = offset + jnp.arange(local_tokens, dtype=jnp.int32)
    earlier = jnp.sum((all_segments[:, None, :] < segments[:, :, None]).astype(jnp.int32), axis=2)
    position = places[None, :] - earlier
    frequency = jnp.power(THETA, -(jnp.arange(HD // 2, dtype=jnp.float32) * 2.0 / HD))
    angles = position.reshape(row_count).astype(jnp.float32)[:, None] * frequency[None, :]
    cosine = jnp.cos(angles)
    sine_table = jnp.sin(angles)
    causal = places[:, None] >= jnp.arange(full_length, dtype=jnp.int32)[None, :]
    allowed = (segments[:, :, None] == all_segments[:, None, :]) & causal[None]
    inputs = tokens.astype(jnp.float32).reshape(row_count, model_width)
    scale_first = rms_scale(inputs)
    normed_first = (inputs * scale_first * gain_first.astype(jnp.float32)).astype(jnp.bfloat16)
    linear = jnp.dot(
        normed_first, qkv_matrix, preferred_element_type=jnp.float32
    ) + qkv_vector.astype(jnp.float32)
    values_local = linear[:, query_width + key_width :].astype(jnp.bfloat16)
    rotated = rotate(
        linear[:, : query_width + key_width].reshape(row_count, head_count + shared_heads, HD),
        cosine,
        sine_table,
    ).astype(jnp.bfloat16)
    queries = rotated[:, :head_count]
    keys_local = rotated[:, head_count:].reshape(row_count, key_width)
    key_values = jnp.concatenate([keys_local, values_local], axis=1).reshape(
        sequences, local_tokens, 2 * key_width
    )
    later_part = jnp.concatenate(
        [out_weight, widen(pick_columns(gate_weight)), pick_columns(up_weight)], axis=1
    )
    down_part = lax.dynamic_slice_in_dim(down_weight, rep_index * part_hidden, part_hidden, 0)
    key_values, later_part, down_part, cotangent = lax.optimization_barrier(
        (key_values, later_part, down_part, cotangent)
    )
    key_values = lax.all_gather(key_values, "shard", axis=1, tiled=True)
    later_set = lax.all_gather(later_part, "shard", axis=0, tiled=True)
    down_matrix = lax.all_gather(down_part, "shard", axis=0, tiled=True)
    grad_output = cotangent.reshape(row_count, model_width)
    grad_output_all = lax.all_gather(grad_output, "rep", axis=0, tiled=True)
    output_matrix = later_set[:, :model_width]
    gate_matrix = later_set[:, model_width : model_width + slice_width]
    up_matrix = later_set[:, model_width + padded_width :]
    queries_grouped = queries.reshape(sequences, local_tokens, shared_heads, group_size, HD)
    keys_heads = key_values[:, :, :key_width].reshape(sequences, full_length, shared_heads, HD)
    values_heads = key_values[:, :, key_width:].reshape(sequences, full_length, shared_heads, HD)
    mixed_blocks, log_blocks = lax.map(
        attend, (split(queries_grouped), split(keys_heads), split(values_heads), split(allowed))
    )
    mixed_heads = mixed_blocks.reshape(row_count, query_width)
    hidden = inputs + jnp.dot(mixed_heads, output_matrix, preferred_element_type=jnp.float32)
    scale_second = rms_scale(hidden)
    normed_second = (hidden * scale_second * gain_second.astype(jnp.float32)).astype(jnp.bfloat16)
    normed_all = lax.all_gather(normed_second, "rep", axis=0, tiled=True)
    gate_linear = jnp.dot(normed_all, gate_matrix, preferred_element_type=jnp.float32)
    up_linear = jnp.dot(normed_all, up_matrix, preferred_element_type=jnp.float32)
    sigmoid_gate = jax.nn.sigmoid(gate_linear)
    activation = (gate_linear * sigmoid_gate * up_linear).astype(jnp.bfloat16)
    grad_activation = times_transposed(grad_output_all, down_matrix)
    gate_slope = sigmoid_gate + gate_linear * sigmoid_gate * (1.0 - sigmoid_gate)
    grad_gate = (grad_activation * up_linear * gate_slope).astype(jnp.bfloat16)
    grad_up = (grad_activation * gate_linear * sigmoid_gate).astype(jnp.bfloat16)
    grad_normed_part = (
        times_transposed(grad_gate, gate_matrix) + times_transposed(grad_up, up_matrix)
    ).astype(jnp.bfloat16)
    grad_normed = lax.psum_scatter(
        grad_normed_part, "rep", scatter_dimension=0, tiled=True
    ).astype(jnp.float32)
    down_grad = inner_rows(activation, grad_output_all).astype(jnp.bfloat16)
    gate_grad = inner_rows(normed_all, grad_gate).astype(jnp.bfloat16)
    up_grad = inner_rows(normed_all, grad_up).astype(jnp.bfloat16)
    down_owned = lax.psum_scatter(down_grad, "shard", scatter_dimension=0, tiled=True)
    second_gain_grad = jnp.sum(grad_normed * hidden * scale_second, axis=0)
    grad_hidden = grad_output.astype(jnp.float32) + norm_back(
        grad_normed, hidden, scale_second, gain_second
    )
    grad_branch = grad_hidden.astype(jnp.bfloat16)
    out_grad = inner_rows(mixed_heads, grad_branch).astype(jnp.bfloat16)
    later_owned = lax.psum_scatter(
        jnp.concatenate([out_grad, widen(gate_grad), up_grad], axis=1),
        "shard",
        scatter_dimension=0,
        tiled=True,
    )
    grad_mixed = times_transposed(grad_branch, output_matrix).astype(jnp.bfloat16)
    grad_mixed = grad_mixed.reshape(sequences, local_tokens, shared_heads, group_size, HD)
    grad_query_blocks, grad_key_blocks, grad_value_blocks = lax.map(
        attend_back,
        (
            split(queries_grouped),
            split(keys_heads),
            split(values_heads),
            split(allowed),
            log_blocks,
            split(grad_mixed),
        ),
    )
    output_part = jnp.dot(activation, down_matrix, preferred_element_type=jnp.float32)
    output = (
        (
            hidden
            + lax.psum_scatter(
                output_part.astype(jnp.bfloat16), "rep", scatter_dimension=0, tiled=True
            ).astype(jnp.float32)
        )
        .astype(jnp.bfloat16)
        .reshape(tokens.shape)
    )
    grad_queries_rot = grad_query_blocks.reshape(row_count, head_count, HD)
    grad_key_values = jnp.concatenate(
        [
            grad_key_blocks.astype(jnp.bfloat16).reshape(sequences, full_length, key_width),
            grad_value_blocks.astype(jnp.bfloat16).reshape(sequences, full_length, key_width),
        ],
        axis=2,
    )
    grad_key_values = lax.psum_scatter(
        grad_key_values, "shard", scatter_dimension=1, tiled=True
    ).reshape(row_count, 2 * key_width)
    grad_keys_sum = grad_key_values[:, :key_width].astype(jnp.float32)
    grad_values = grad_key_values[:, key_width:]
    grad_queries = (
        rotate(grad_queries_rot, cosine, -sine_table)
        .astype(jnp.bfloat16)
        .reshape(row_count, query_width)
    )
    grad_keys = (
        rotate(grad_keys_sum.reshape(row_count, shared_heads, HD), cosine, -sine_table)
        .astype(jnp.bfloat16)
        .reshape(row_count, key_width)
    )
    grad_qkv = jnp.concatenate([grad_queries, grad_keys, grad_values], axis=1)
    qkv_grad = inner_rows(normed_first, grad_qkv).astype(jnp.bfloat16)
    bias_grad = jnp.sum(grad_qkv.astype(jnp.float32), axis=0)
    grad_first = times_transposed(grad_qkv, qkv_matrix)
    first_gain_grad = jnp.sum(grad_first * inputs * scale_first, axis=0)
    tokens_grad = (
        (grad_hidden + norm_back(grad_first, inputs, scale_first, gain_first))
        .astype(jnp.bfloat16)
        .reshape(tokens.shape)
    )
    small_grad = jnp.concatenate(
        [
            piece.astype(jnp.bfloat16).reshape(shards, -1)
            for piece in (
                first_gain_grad,
                second_gain_grad,
                bias_grad[:query_width],
                bias_grad[query_width : query_width + key_width],
                bias_grad[query_width + key_width :],
            )
        ],
        axis=1,
    )
    extra_rows = small.shape[0]
    small_grad = jnp.pad(
        small_grad, ((0, 0), (0, extra_rows * qkv_width - small_grad.shape[1]))
    ).reshape(shards, extra_rows, qkv_width)
    first_owned = lax.psum_scatter(
        jnp.concatenate([qkv_grad.reshape(shards, own_rows, qkv_width), small_grad], axis=1),
        "shard",
        scatter_dimension=0,
        tiled=False,
    )
    first_owned, out_owned = lax.psum((first_owned, later_owned[:, :model_width]), "rep")
    first_owned = first_owned.astype(jnp.float32)
    hidden_set = lax.all_gather(later_owned[:, model_width:], "rep", axis=0, tiled=False)
    down_set = lax.all_gather(down_owned, "rep", axis=0, tiled=True)

    def spread_columns(parts):
        grouped = parts.reshape(reps, own_rows, shards, part_hidden)
        return grouped.transpose(1, 2, 0, 3).reshape(own_rows, hidden_width).astype(jnp.float32)

    small_owned = first_owned[own_rows:].reshape(-1)
    small_outs = [small_owned[starts[i] : starts[i] + sizes[i]] for i in range(len(sizes))]
    return (
        output,
        tokens_grad,
        small_outs[0],
        first_owned[:own_rows, :query_width],
        small_outs[2],
        first_owned[:own_rows, query_width : query_width + key_width],
        small_outs[3],
        first_owned[:own_rows, query_width + key_width :],
        small_outs[4],
        out_owned.astype(jnp.float32),
        small_outs[1],
        spread_columns(hidden_set[:, :, :slice_width]),
        spread_columns(hidden_set[:, :, padded_width:]),
        down_set.astype(jnp.float32),
    )


def solution(mesh):
    placed = (
        P("rep", "shard", None),
        P("rep", "shard"),
        P("shard"),
        P("shard", None),
        P("shard"),
        P("shard", None),
        P("shard"),
        P("shard", None),
        P("shard"),
        P("shard", None),
        P("shard"),
        P("shard", None),
        P("shard", None),
        P("shard", None),
        P("rep", "shard", None),
    )
    return jax.shard_map(
        functools.partial(on_device, reps=mesh.shape["rep"], shards=mesh.shape["shard"]),
        mesh=mesh,
        in_specs=placed,
        out_specs=(
            P("rep", "shard", None),
            P("rep", "shard", None),
            P("shard"),
            P("shard", None),
            P("shard"),
            P("shard", None),
            P("shard"),
            P("shard", None),
            P("shard"),
            P("shard", None),
            P("shard"),
            P("shard", None),
            P("shard", None),
            P("shard", None),
        ),
        check_vma=False,
    )
```

```python
import functools
import math

import jax
import jax.numpy as jnp
from jax import lax
from jax.sharding import PartitionSpec as P

HD = 64


EPSILON = 1e-06
THETA = 1000000.0
MASKED = -1000000000.0


def rms_scale(values):
    return lax.rsqrt(jnp.mean(values * values, axis=-1, keepdims=True) + EPSILON)


def rotate(values, cosine, sine_table):
    half_size = values.shape[-1] // 2
    first_half = values[..., :half_size]
    second_half = values[..., half_size:]
    cosine = cosine[:, None, :]
    sine_table = sine_table[:, None, :]
    return jnp.concatenate(
        [
            first_half * cosine - second_half * sine_table,
            second_half * cosine + first_half * sine_table,
        ],
        axis=-1,
    )


def inner_rows(left_side, right_side):
    return lax.dot_general(
        left_side, right_side, (((0,), (0,)), ((), ())), preferred_element_type=jnp.float32
    )


def times_transposed(left_side, right_side):
    return lax.dot_general(
        left_side, right_side, (((1,), (1,)), ((), ())), preferred_element_type=jnp.float32
    )


def norm_back(grad_normed, values, scale_rows, gain_value):
    normal = values * scale_rows
    grad_scaled = grad_normed * gain_value.astype(jnp.float32)
    return scale_rows * (
        grad_scaled - normal * jnp.mean(grad_scaled * normal, axis=-1, keepdims=True)
    )


def masked_scores(query_block, key_block, mask_block):
    raw_scores = jnp.einsum(
        "bqkgd,bskd->bkgqs", query_block, key_block, preferred_element_type=jnp.float32
    ) * HD ** (-0.5)
    return jnp.where(mask_block[:, None, None], raw_scores, MASKED)


def attend(items):
    query_block, key_block, value_block, mask_block = items
    scores = masked_scores(query_block, key_block, mask_block)
    row_max = jnp.max(scores, axis=-1, keepdims=True)
    weights = jnp.exp(scores - row_max)
    row_total = jnp.sum(weights, axis=-1, keepdims=True)
    probs = (weights / row_total).astype(jnp.bfloat16)
    mixed = jnp.einsum("bkgqs,bskd->bqkgd", probs, value_block, preferred_element_type=jnp.float32)
    return (mixed.astype(jnp.bfloat16), row_max + jnp.log(row_total))


def attend_back(items):
    query_block, key_block, value_block, mask_block, log_block, grad_block = items
    scores = masked_scores(query_block, key_block, mask_block)
    probs_full = jnp.exp(scores - log_block)
    grad_probs = jnp.einsum(
        "bqkgd,bskd->bkgqs", grad_block, value_block, preferred_element_type=jnp.float32
    )
    row_delta = jnp.sum(probs_full * grad_probs, axis=-1, keepdims=True)
    grad_scores = (probs_full * (grad_probs - row_delta)).astype(jnp.bfloat16)
    grad_query = jnp.einsum(
        "bkgqs,bskd->bqkgd", grad_scores, key_block, preferred_element_type=jnp.float32
    ) * HD ** (-0.5)
    grad_key = jnp.einsum(
        "bkgqs,bqkgd->bskd", grad_scores, query_block, preferred_element_type=jnp.float32
    ) * HD ** (-0.5)
    grad_value = jnp.einsum(
        "bkgqs,bqkgd->bskd",
        probs_full.astype(jnp.bfloat16),
        grad_block,
        preferred_element_type=jnp.float32,
    )
    return (grad_query, grad_key, grad_value)


def pack_rows(pieces, width):
    flat = jnp.concatenate(pieces)
    rows = -(-flat.shape[0] // (8 * width)) * 8
    return jnp.pad(flat, (0, rows * width - flat.shape[0])).reshape(rows, width)


def partner_swap(values, bit, reps):
    return lax.ppermute(values, "rep", [(i, i ^ bit) for i in range(reps)])


def rep_bits(reps):
    return [1 << i for i in range(reps.bit_length() - 1)]


def rep_places(reps):
    places = [0]
    for bit in reversed(rep_bits(reps)):
        places = places + [place ^ bit for place in places]
    return places


def rep_gather(values, reps):
    for bit in reversed(rep_bits(reps)):
        values = jnp.concatenate([values, partner_swap(values, bit, reps)], axis=0)
    return values


def rep_scatter(values, reps):
    for bit in rep_bits(reps):
        half = values.shape[0] // 2
        received = partner_swap(values[half:].astype(jnp.bfloat16), bit, reps)
        values = values[:half].astype(jnp.float32) + received.astype(jnp.float32)
    return values.astype(jnp.float32)


def rep_sum(values, reps):
    for bit in rep_bits(reps):
        sent = values.astype(jnp.bfloat16)
        received = partner_swap(sent, bit, reps)
        values = sent.astype(jnp.float32) + received.astype(jnp.float32)
    return values


def rep_ordered(values, reps, rep_index):
    gathered = rep_gather(values[None], reps)
    where_is = [0] * reps
    for spot, place in enumerate(rep_places(reps)):
        where_is[place] = spot
    table = jnp.asarray(where_is, dtype=jnp.int32)
    return jnp.stack(
        [
            lax.dynamic_index_in_dim(gathered, table[rep_index ^ i], 0, keepdims=False)
            for i in range(reps)
        ]
    )


def on_device(
    tokens,
    segments,
    first_gain,
    query_weight,
    query_bias,
    key_weight,
    key_bias,
    value_weight,
    value_bias,
    out_weight,
    second_gain,
    gate_weight,
    up_weight,
    down_weight,
    cotangent,
    reps,
    shards,
):
    sequences, local_tokens, model_width = tokens.shape
    row_count = sequences * local_tokens
    own_rows = first_gain.shape[0]
    query_width = query_weight.shape[1]
    key_width = key_weight.shape[1]
    hidden_width = gate_weight.shape[1]
    own_hidden = down_weight.shape[0]
    part_hidden = own_hidden // reps
    slice_width = part_hidden * shards
    padded_width = -(-slice_width // 128) * 128
    qkv_width = query_width + 2 * key_width
    head_count = query_width // HD
    shared_heads = key_width // HD
    group_size = head_count // shared_heads
    block_seqs = math.gcd(sequences, max(1, 512 // local_tokens))
    block_count = sequences // block_seqs
    rep_index = lax.axis_index("rep")

    def split(values):
        return values.reshape((block_count, block_seqs) + values.shape[1:])

    def pick_columns(weight):
        grouped = weight.reshape(own_rows, shards, reps, part_hidden)
        picked = lax.dynamic_index_in_dim(grouped, rep_index, 2, keepdims=False)
        return picked.reshape(own_rows, slice_width)

    def widen(values):
        return jnp.pad(values, ((0, 0), (0, padded_width - slice_width)))

    small = pack_rows(
        [
            first_gain,
            second_gain,
            query_bias,
            key_bias,
            value_bias,
            segments.reshape(-1).astype(jnp.bfloat16),
        ],
        qkv_width,
    )
    qkv_part = jnp.concatenate([query_weight, key_weight, value_weight], axis=1)
    first_set = lax.all_gather(
        jnp.concatenate([qkv_part, small], axis=0), "shard", axis=0, tiled=False
    )
    qkv_matrix = first_set[:, :own_rows].reshape(model_width, qkv_width)
    small_set = first_set[:, own_rows:].reshape(shards, -1)
    sizes = [own_rows, own_rows, own_rows, key_bias.shape[0], value_bias.shape[0]]
    starts = [sum(sizes[:i]) for i in range(len(sizes) + 1)]
    gain_first, gain_second, query_vector, key_vector, value_vector = [
        small_set[:, starts[i] : starts[i] + sizes[i]].reshape(-1) for i in range(len(sizes))
    ]
    qkv_vector = jnp.concatenate([query_vector, key_vector, value_vector])
    all_segments = (
        small_set[:, starts[-1] : starts[-1] + row_count]
        .reshape(shards, sequences, local_tokens)
        .transpose(1, 0, 2)
        .reshape(sequences, shards * local_tokens)
        .astype(jnp.int32)
    )
    full_length = all_segments.shape[1]
    offset = lax.axis_index("shard") * local_tokens
    places = offset + jnp.arange(local_tokens, dtype=jnp.int32)
    earlier = jnp.sum((all_segments[:, None, :] < segments[:, :, None]).astype(jnp.int32), axis=2)
    position = places[None, :] - earlier
    frequency = jnp.power(THETA, -(jnp.arange(HD // 2, dtype=jnp.float32) * 2.0 / HD))
    angles = position.reshape(row_count).astype(jnp.float32)[:, None] * frequency[None, :]
    cosine = jnp.cos(angles)
    sine_table = jnp.sin(angles)
    causal = places[:, None] >= jnp.arange(full_length, dtype=jnp.int32)[None, :]
    allowed = (segments[:, :, None] == all_segments[:, None, :]) & causal[None]
    inputs = tokens.astype(jnp.float32).reshape(row_count, model_width)
    scale_first = rms_scale(inputs)
    normed_first = (inputs * scale_first * gain_first.astype(jnp.float32)).astype(jnp.bfloat16)
    linear = jnp.dot(
        normed_first, qkv_matrix, preferred_element_type=jnp.float32
    ) + qkv_vector.astype(jnp.float32)
    values_local = linear[:, query_width + key_width :].astype(jnp.bfloat16)
    rotated = rotate(
        linear[:, : query_width + key_width].reshape(row_count, head_count + shared_heads, HD),
        cosine,
        sine_table,
    ).astype(jnp.bfloat16)
    queries = rotated[:, :head_count]
    keys_local = rotated[:, head_count:].reshape(row_count, key_width)
    key_values = jnp.concatenate([keys_local, values_local], axis=1).reshape(
        sequences, local_tokens, 2 * key_width
    )
    later_part = jnp.concatenate(
        [out_weight, widen(pick_columns(gate_weight)), pick_columns(up_weight)], axis=1
    )
    down_part = lax.dynamic_slice_in_dim(down_weight, rep_index * part_hidden, part_hidden, 0)
    key_values, later_part, down_part = lax.optimization_barrier(
        (key_values, later_part, down_part)
    )
    key_values = lax.all_gather(key_values, "shard", axis=1, tiled=True)
    later_set = lax.all_gather(later_part, "shard", axis=0, tiled=True)
    down_matrix = lax.all_gather(down_part, "shard", axis=0, tiled=True)
    grad_output = cotangent.reshape(row_count, model_width)
    grad_output_all = rep_gather(grad_output, reps)
    output_matrix = later_set[:, :model_width]
    gate_matrix = later_set[:, model_width : model_width + slice_width]
    up_matrix = later_set[:, model_width + padded_width :]
    queries_grouped = queries.reshape(sequences, local_tokens, shared_heads, group_size, HD)
    keys_heads = key_values[:, :, :key_width].reshape(sequences, full_length, shared_heads, HD)
    values_heads = key_values[:, :, key_width:].reshape(sequences, full_length, shared_heads, HD)
    mixed_blocks, log_blocks = lax.map(
        attend, (split(queries_grouped), split(keys_heads), split(values_heads), split(allowed))
    )
    mixed_heads = mixed_blocks.reshape(row_count, query_width)
    hidden = inputs + jnp.dot(mixed_heads, output_matrix, preferred_element_type=jnp.float32)
    scale_second = rms_scale(hidden)
    normed_second = (hidden * scale_second * gain_second.astype(jnp.float32)).astype(jnp.bfloat16)
    normed_all = rep_gather(normed_second, reps)
    gate_linear = jnp.dot(normed_all, gate_matrix, preferred_element_type=jnp.float32)
    up_linear = jnp.dot(normed_all, up_matrix, preferred_element_type=jnp.float32)
    sigmoid_gate = jax.nn.sigmoid(gate_linear)
    activation = (gate_linear * sigmoid_gate * up_linear).astype(jnp.bfloat16)
    grad_activation = times_transposed(grad_output_all, down_matrix)
    gate_slope = sigmoid_gate + gate_linear * sigmoid_gate * (1.0 - sigmoid_gate)
    grad_gate = (grad_activation * up_linear * gate_slope).astype(jnp.bfloat16)
    grad_up = (grad_activation * gate_linear * sigmoid_gate).astype(jnp.bfloat16)
    grad_normed_part = (
        times_transposed(grad_gate, gate_matrix) + times_transposed(grad_up, up_matrix)
    ).astype(jnp.bfloat16)
    grad_normed = rep_scatter(grad_normed_part, reps)
    down_grad = inner_rows(activation, grad_output_all).astype(jnp.bfloat16)
    gate_grad = inner_rows(normed_all, grad_gate).astype(jnp.bfloat16)
    up_grad = inner_rows(normed_all, grad_up).astype(jnp.bfloat16)
    second_gain_grad = jnp.sum(grad_normed * hidden * scale_second, axis=0)
    grad_hidden = grad_output.astype(jnp.float32) + norm_back(
        grad_normed, hidden, scale_second, gain_second
    )
    grad_branch = grad_hidden.astype(jnp.bfloat16)
    out_grad = inner_rows(mixed_heads, grad_branch).astype(jnp.bfloat16)
    later_grad = jnp.concatenate([out_grad, widen(gate_grad), up_grad], axis=1)
    grad_mixed = times_transposed(grad_branch, output_matrix).astype(jnp.bfloat16)
    grad_mixed, later_grad, down_grad = lax.optimization_barrier(
        (grad_mixed, later_grad, down_grad)
    )
    down_owned = lax.psum_scatter(down_grad, "shard", scatter_dimension=0, tiled=True)
    later_owned = lax.psum_scatter(later_grad, "shard", scatter_dimension=0, tiled=True)
    grad_mixed = grad_mixed.reshape(sequences, local_tokens, shared_heads, group_size, HD)
    grad_query_blocks, grad_key_blocks, grad_value_blocks = lax.map(
        attend_back,
        (
            split(queries_grouped),
            split(keys_heads),
            split(values_heads),
            split(allowed),
            log_blocks,
            split(grad_mixed),
        ),
    )
    output_part = jnp.dot(activation, down_matrix, preferred_element_type=jnp.float32)
    output = (
        (
            hidden
            + rep_scatter(output_part.astype(jnp.bfloat16), reps)
        )
        .astype(jnp.bfloat16)
        .reshape(tokens.shape)
    )
    grad_queries_rot = grad_query_blocks.reshape(row_count, head_count, HD)
    grad_key_values = jnp.concatenate(
        [
            grad_key_blocks.astype(jnp.bfloat16).reshape(sequences, full_length, key_width),
            grad_value_blocks.astype(jnp.bfloat16).reshape(sequences, full_length, key_width),
        ],
        axis=2,
    )
    grad_key_values = lax.psum_scatter(
        grad_key_values, "shard", scatter_dimension=1, tiled=True
    ).reshape(row_count, 2 * key_width)
    grad_keys_sum = grad_key_values[:, :key_width].astype(jnp.float32)
    grad_values = grad_key_values[:, key_width:]
    grad_queries = (
        rotate(grad_queries_rot, cosine, -sine_table)
        .astype(jnp.bfloat16)
        .reshape(row_count, query_width)
    )
    grad_keys = (
        rotate(grad_keys_sum.reshape(row_count, shared_heads, HD), cosine, -sine_table)
        .astype(jnp.bfloat16)
        .reshape(row_count, key_width)
    )
    grad_qkv = jnp.concatenate([grad_queries, grad_keys, grad_values], axis=1)
    qkv_grad = inner_rows(normed_first, grad_qkv).astype(jnp.bfloat16)
    bias_grad = jnp.sum(grad_qkv.astype(jnp.float32), axis=0)
    grad_first = times_transposed(grad_qkv, qkv_matrix)
    first_gain_grad = jnp.sum(grad_first * inputs * scale_first, axis=0)
    tokens_grad = (
        (grad_hidden + norm_back(grad_first, inputs, scale_first, gain_first))
        .astype(jnp.bfloat16)
        .reshape(tokens.shape)
    )
    small_grad = jnp.concatenate(
        [
            piece.astype(jnp.bfloat16).reshape(shards, -1)
            for piece in (
                first_gain_grad,
                second_gain_grad,
                bias_grad[:query_width],
                bias_grad[query_width : query_width + key_width],
                bias_grad[query_width + key_width :],
            )
        ],
        axis=1,
    )
    extra_rows = small.shape[0]
    small_grad = jnp.pad(
        small_grad, ((0, 0), (0, extra_rows * qkv_width - small_grad.shape[1]))
    ).reshape(shards, extra_rows, qkv_width)
    first_owned = lax.psum_scatter(
        jnp.concatenate([qkv_grad.reshape(shards, own_rows, qkv_width), small_grad], axis=1),
        "shard",
        scatter_dimension=0,
        tiled=False,
    )
    first_owned = rep_sum(first_owned, reps)
    out_owned = rep_sum(later_owned[:, :model_width], reps)
    hidden_set = rep_ordered(later_owned[:, model_width:], reps, rep_index)
    down_set = rep_ordered(down_owned, reps, rep_index).reshape(own_hidden, model_width)

    def spread_columns(parts):
        grouped = parts.reshape(reps, own_rows, shards, part_hidden)
        return grouped.transpose(1, 2, 0, 3).reshape(own_rows, hidden_width).astype(jnp.float32)

    small_owned = first_owned[own_rows:].reshape(-1)
    small_outs = [small_owned[starts[i] : starts[i] + sizes[i]] for i in range(len(sizes))]
    return (
        output,
        tokens_grad,
        small_outs[0],
        first_owned[:own_rows, :query_width],
        small_outs[2],
        first_owned[:own_rows, query_width : query_width + key_width],
        small_outs[3],
        first_owned[:own_rows, query_width + key_width :],
        small_outs[4],
        out_owned.astype(jnp.float32),
        small_outs[1],
        spread_columns(hidden_set[:, :, :slice_width]),
        spread_columns(hidden_set[:, :, padded_width:]),
        down_set.astype(jnp.float32),
    )


def solution(mesh):
    placed = (
        P("rep", "shard", None),
        P("rep", "shard"),
        P("shard"),
        P("shard", None),
        P("shard"),
        P("shard", None),
        P("shard"),
        P("shard", None),
        P("shard"),
        P("shard", None),
        P("shard"),
        P("shard", None),
        P("shard", None),
        P("shard", None),
        P("rep", "shard", None),
    )
    return jax.shard_map(
        functools.partial(on_device, reps=mesh.shape["rep"], shards=mesh.shape["shard"]),
        mesh=mesh,
        in_specs=placed,
        out_specs=(
            P("rep", "shard", None),
            P("rep", "shard", None),
            P("shard"),
            P("shard", None),
            P("shard"),
            P("shard", None),
            P("shard"),
            P("shard", None),
            P("shard"),
            P("shard", None),
            P("shard"),
            P("shard", None),
            P("shard", None),
            P("shard", None),
        ),
        check_vma=False,
    )
```

```python
import functools
import math

import jax
import jax.numpy as jnp
from jax import lax
from jax.sharding import PartitionSpec as P

HD = 64


EPSILON = 1e-06
THETA = 1000000.0
MASKED = -1000000000.0


def rms_scale(values):
    return lax.rsqrt(jnp.mean(values * values, axis=-1, keepdims=True) + EPSILON)


def rotate(values, cosine, sine_table):
    half_size = values.shape[-1] // 2
    first_half = values[..., :half_size]
    second_half = values[..., half_size:]
    cosine = cosine[:, None, :]
    sine_table = sine_table[:, None, :]
    return jnp.concatenate(
        [
            first_half * cosine - second_half * sine_table,
            second_half * cosine + first_half * sine_table,
        ],
        axis=-1,
    )


def inner_rows(left_side, right_side):
    return lax.dot_general(
        left_side, right_side, (((0,), (0,)), ((), ())), preferred_element_type=jnp.float32
    )


def times_transposed(left_side, right_side):
    return lax.dot_general(
        left_side, right_side, (((1,), (1,)), ((), ())), preferred_element_type=jnp.float32
    )


def norm_back(grad_normed, values, scale_rows, gain_value):
    normal = values * scale_rows
    grad_scaled = grad_normed * gain_value.astype(jnp.float32)
    return scale_rows * (
        grad_scaled - normal * jnp.mean(grad_scaled * normal, axis=-1, keepdims=True)
    )


def masked_scores(query_block, key_block, mask_block):
    raw_scores = jnp.einsum(
        "bqkgd,bskd->bkgqs", query_block, key_block, preferred_element_type=jnp.float32
    ) * HD ** (-0.5)
    return jnp.where(mask_block[:, None, None], raw_scores, MASKED)


def attend(items):
    query_block, key_block, value_block, mask_block = items
    scores = masked_scores(query_block, key_block, mask_block)
    row_max = jnp.max(scores, axis=-1, keepdims=True)
    weights = jnp.exp(scores - row_max)
    row_total = jnp.sum(weights, axis=-1, keepdims=True)
    probs = (weights / row_total).astype(jnp.bfloat16)
    mixed = jnp.einsum("bkgqs,bskd->bqkgd", probs, value_block, preferred_element_type=jnp.float32)
    return (mixed.astype(jnp.bfloat16), row_max + jnp.log(row_total))


def attend_back(items):
    query_block, key_block, value_block, mask_block, log_block, grad_block = items
    scores = masked_scores(query_block, key_block, mask_block)
    probs_full = jnp.exp(scores - log_block)
    grad_probs = jnp.einsum(
        "bqkgd,bskd->bkgqs", grad_block, value_block, preferred_element_type=jnp.float32
    )
    row_delta = jnp.sum(probs_full * grad_probs, axis=-1, keepdims=True)
    grad_scores = (probs_full * (grad_probs - row_delta)).astype(jnp.bfloat16)
    grad_query = jnp.einsum(
        "bkgqs,bskd->bqkgd", grad_scores, key_block, preferred_element_type=jnp.float32
    ) * HD ** (-0.5)
    grad_key = jnp.einsum(
        "bkgqs,bqkgd->bskd", grad_scores, query_block, preferred_element_type=jnp.float32
    ) * HD ** (-0.5)
    grad_value = jnp.einsum(
        "bkgqs,bqkgd->bskd",
        probs_full.astype(jnp.bfloat16),
        grad_block,
        preferred_element_type=jnp.float32,
    )
    return (grad_query, grad_key, grad_value)


def pack_rows(pieces, width):
    flat = jnp.concatenate(pieces)
    rows = -(-flat.shape[0] // (8 * width)) * 8
    return jnp.pad(flat, (0, rows * width - flat.shape[0])).reshape(rows, width)


def partner_swap(values, bit, reps):
    return lax.ppermute(values, "rep", [(i, i ^ bit) for i in range(reps)])


def rep_bits(reps):
    return [1 << i for i in range(reps.bit_length() - 1)]


def rep_places(reps):
    places = [0]
    for bit in reversed(rep_bits(reps)):
        places = places + [place ^ bit for place in places]
    return places


def rep_gather(values, reps):
    for bit in reversed(rep_bits(reps)):
        values = jnp.concatenate([values, partner_swap(values, bit, reps)], axis=0)
    return values


def rep_scatter(values, reps):
    for bit in rep_bits(reps):
        half = values.shape[0] // 2
        received = partner_swap(values[half:].astype(jnp.bfloat16), bit, reps)
        values = values[:half].astype(jnp.float32) + received.astype(jnp.float32)
    return values.astype(jnp.float32)


def rep_sum(values, reps):
    for bit in rep_bits(reps):
        sent = values.astype(jnp.bfloat16)
        received = partner_swap(sent, bit, reps)
        values = sent.astype(jnp.float32) + received.astype(jnp.float32)
    return values


def rep_ordered(values, reps, rep_index):
    gathered = rep_gather(values[None], reps)
    where_is = [0] * reps
    for spot, place in enumerate(rep_places(reps)):
        where_is[place] = spot
    table = jnp.asarray(where_is, dtype=jnp.int32)
    return jnp.stack(
        [
            lax.dynamic_index_in_dim(gathered, table[rep_index ^ i], 0, keepdims=False)
            for i in range(reps)
        ]
    )


def on_device(
    tokens,
    segments,
    first_gain,
    query_weight,
    query_bias,
    key_weight,
    key_bias,
    value_weight,
    value_bias,
    out_weight,
    second_gain,
    gate_weight,
    up_weight,
    down_weight,
    cotangent,
    reps,
    shards,
):
    sequences, local_tokens, model_width = tokens.shape
    row_count = sequences * local_tokens
    own_rows = first_gain.shape[0]
    query_width = query_weight.shape[1]
    key_width = key_weight.shape[1]
    hidden_width = gate_weight.shape[1]
    own_hidden = down_weight.shape[0]
    part_hidden = own_hidden // reps
    slice_width = part_hidden * shards
    padded_width = -(-slice_width // 128) * 128
    qkv_width = query_width + 2 * key_width
    head_count = query_width // HD
    shared_heads = key_width // HD
    group_size = head_count // shared_heads
    block_seqs = math.gcd(sequences, max(1, 512 // local_tokens))
    block_count = sequences // block_seqs
    rep_index = lax.axis_index("rep")

    def split(values):
        return values.reshape((block_count, block_seqs) + values.shape[1:])

    def pick_columns(weight):
        grouped = weight.reshape(own_rows, shards, reps, part_hidden)
        picked = lax.dynamic_index_in_dim(grouped, rep_index, 2, keepdims=False)
        return picked.reshape(own_rows, slice_width)

    def widen(values):
        return jnp.pad(values, ((0, 0), (0, padded_width - slice_width)))

    small = pack_rows(
        [
            first_gain,
            second_gain,
            query_bias,
            key_bias,
            value_bias,
            segments.reshape(-1).astype(jnp.bfloat16),
        ],
        qkv_width,
    )
    qkv_part = jnp.concatenate([query_weight, key_weight, value_weight], axis=1)
    first_set = lax.all_gather(
        jnp.concatenate([qkv_part, small], axis=0), "shard", axis=0, tiled=False
    )
    qkv_matrix = first_set[:, :own_rows].reshape(model_width, qkv_width)
    small_set = first_set[:, own_rows:].reshape(shards, -1)
    sizes = [own_rows, own_rows, own_rows, key_bias.shape[0], value_bias.shape[0]]
    starts = [sum(sizes[:i]) for i in range(len(sizes) + 1)]
    gain_first, gain_second, query_vector, key_vector, value_vector = [
        small_set[:, starts[i] : starts[i] + sizes[i]].reshape(-1) for i in range(len(sizes))
    ]
    qkv_vector = jnp.concatenate([query_vector, key_vector, value_vector])
    all_segments = (
        small_set[:, starts[-1] : starts[-1] + row_count]
        .reshape(shards, sequences, local_tokens)
        .transpose(1, 0, 2)
        .reshape(sequences, shards * local_tokens)
        .astype(jnp.int32)
    )
    full_length = all_segments.shape[1]
    offset = lax.axis_index("shard") * local_tokens
    places = offset + jnp.arange(local_tokens, dtype=jnp.int32)
    earlier = jnp.sum((all_segments[:, None, :] < segments[:, :, None]).astype(jnp.int32), axis=2)
    position = places[None, :] - earlier
    frequency = jnp.power(THETA, -(jnp.arange(HD // 2, dtype=jnp.float32) * 2.0 / HD))
    angles = position.reshape(row_count).astype(jnp.float32)[:, None] * frequency[None, :]
    cosine = jnp.cos(angles)
    sine_table = jnp.sin(angles)
    causal = places[:, None] >= jnp.arange(full_length, dtype=jnp.int32)[None, :]
    allowed = (segments[:, :, None] == all_segments[:, None, :]) & causal[None]
    inputs = tokens.astype(jnp.float32).reshape(row_count, model_width)
    scale_first = rms_scale(inputs)
    normed_first = (inputs * scale_first * gain_first.astype(jnp.float32)).astype(jnp.bfloat16)
    linear = jnp.dot(
        normed_first, qkv_matrix, preferred_element_type=jnp.float32
    ) + qkv_vector.astype(jnp.float32)
    values_local = linear[:, query_width + key_width :].astype(jnp.bfloat16)
    rotated = rotate(
        linear[:, : query_width + key_width].reshape(row_count, head_count + shared_heads, HD),
        cosine,
        sine_table,
    ).astype(jnp.bfloat16)
    queries = rotated[:, :head_count]
    keys_local = rotated[:, head_count:].reshape(row_count, key_width)
    key_values = jnp.concatenate([keys_local, values_local], axis=1).reshape(
        sequences, local_tokens, 2 * key_width
    )
    later_part = jnp.concatenate(
        [out_weight, widen(pick_columns(gate_weight)), pick_columns(up_weight)], axis=1
    )
    down_part = lax.dynamic_slice_in_dim(down_weight, rep_index * part_hidden, part_hidden, 0)
    key_values, later_part, down_part = lax.optimization_barrier(
        (key_values, later_part, down_part)
    )
    key_values = lax.all_gather(key_values, "shard", axis=1, tiled=True)
    later_set = lax.all_gather(later_part, "shard", axis=0, tiled=True)
    down_matrix = lax.all_gather(down_part, "shard", axis=0, tiled=True)
    grad_output = cotangent.reshape(row_count, model_width)
    grad_output_all = rep_gather(grad_output, reps)
    output_matrix = later_set[:, :model_width]
    gate_matrix = later_set[:, model_width : model_width + slice_width]
    up_matrix = later_set[:, model_width + padded_width :]
    queries_grouped = queries.reshape(sequences, local_tokens, shared_heads, group_size, HD)
    keys_heads = key_values[:, :, :key_width].reshape(sequences, full_length, shared_heads, HD)
    values_heads = key_values[:, :, key_width:].reshape(sequences, full_length, shared_heads, HD)
    mixed_blocks, log_blocks = lax.map(
        attend, (split(queries_grouped), split(keys_heads), split(values_heads), split(allowed))
    )
    mixed_heads = mixed_blocks.reshape(row_count, query_width)
    hidden = inputs + jnp.dot(mixed_heads, output_matrix, preferred_element_type=jnp.float32)
    scale_second = rms_scale(hidden)
    normed_second = (hidden * scale_second * gain_second.astype(jnp.float32)).astype(jnp.bfloat16)
    normed_all = rep_gather(normed_second, reps)
    gate_linear = jnp.dot(normed_all, gate_matrix, preferred_element_type=jnp.float32)
    up_linear = jnp.dot(normed_all, up_matrix, preferred_element_type=jnp.float32)
    sigmoid_gate = jax.nn.sigmoid(gate_linear)
    activation = (gate_linear * sigmoid_gate * up_linear).astype(jnp.bfloat16)
    grad_activation = times_transposed(grad_output_all, down_matrix)
    gate_slope = sigmoid_gate + gate_linear * sigmoid_gate * (1.0 - sigmoid_gate)
    grad_gate = (grad_activation * up_linear * gate_slope).astype(jnp.bfloat16)
    grad_up = (grad_activation * gate_linear * sigmoid_gate).astype(jnp.bfloat16)
    grad_normed_part = (
        times_transposed(grad_gate, gate_matrix) + times_transposed(grad_up, up_matrix)
    ).astype(jnp.bfloat16)
    grad_normed = rep_scatter(grad_normed_part, reps)
    down_grad = inner_rows(activation, grad_output_all).astype(jnp.bfloat16)
    gate_grad = inner_rows(normed_all, grad_gate).astype(jnp.bfloat16)
    up_grad = inner_rows(normed_all, grad_up).astype(jnp.bfloat16)
    second_gain_grad = jnp.sum(grad_normed * hidden * scale_second, axis=0)
    grad_hidden = grad_output.astype(jnp.float32) + norm_back(
        grad_normed, hidden, scale_second, gain_second
    )
    grad_branch = grad_hidden.astype(jnp.bfloat16)
    out_grad = inner_rows(mixed_heads, grad_branch).astype(jnp.bfloat16)
    later_grad = jnp.concatenate([out_grad, widen(gate_grad), up_grad], axis=1)
    grad_mixed = times_transposed(grad_branch, output_matrix).astype(jnp.bfloat16)
    grad_mixed, later_grad, down_grad = lax.optimization_barrier(
        (grad_mixed, later_grad, down_grad)
    )
    down_owned = lax.psum_scatter(down_grad, "shard", scatter_dimension=0, tiled=True)
    later_owned = lax.psum_scatter(later_grad, "shard", scatter_dimension=0, tiled=True)
    grad_mixed = grad_mixed.reshape(sequences, local_tokens, shared_heads, group_size, HD)
    grad_query_blocks, grad_key_blocks, grad_value_blocks = lax.map(
        attend_back,
        (
            split(queries_grouped),
            split(keys_heads),
            split(values_heads),
            split(allowed),
            log_blocks,
            split(grad_mixed),
        ),
    )
    output_part = jnp.dot(activation, down_matrix, preferred_element_type=jnp.float32)
    output = (
        (
            hidden
            + rep_scatter(output_part.astype(jnp.bfloat16), reps)
        )
        .astype(jnp.bfloat16)
        .reshape(tokens.shape)
    )
    grad_queries_rot = grad_query_blocks.reshape(row_count, head_count, HD)
    grad_key_values = jnp.concatenate(
        [
            grad_key_blocks.astype(jnp.bfloat16).reshape(sequences, full_length, key_width),
            grad_value_blocks.astype(jnp.bfloat16).reshape(sequences, full_length, key_width),
        ],
        axis=2,
    )
    grad_key_values, later_owned, down_owned = lax.optimization_barrier(
        (grad_key_values, later_owned, down_owned)
    )
    grad_key_values = lax.psum_scatter(
        grad_key_values, "shard", scatter_dimension=1, tiled=True
    ).reshape(row_count, 2 * key_width)
    grad_keys_sum = grad_key_values[:, :key_width].astype(jnp.float32)
    grad_values = grad_key_values[:, key_width:]
    grad_queries = (
        rotate(grad_queries_rot, cosine, -sine_table)
        .astype(jnp.bfloat16)
        .reshape(row_count, query_width)
    )
    grad_keys = (
        rotate(grad_keys_sum.reshape(row_count, shared_heads, HD), cosine, -sine_table)
        .astype(jnp.bfloat16)
        .reshape(row_count, key_width)
    )
    grad_qkv = jnp.concatenate([grad_queries, grad_keys, grad_values], axis=1)
    qkv_grad = inner_rows(normed_first, grad_qkv).astype(jnp.bfloat16)
    bias_grad = jnp.sum(grad_qkv.astype(jnp.float32), axis=0)
    grad_first = times_transposed(grad_qkv, qkv_matrix)
    first_gain_grad = jnp.sum(grad_first * inputs * scale_first, axis=0)
    tokens_grad = (
        (grad_hidden + norm_back(grad_first, inputs, scale_first, gain_first))
        .astype(jnp.bfloat16)
        .reshape(tokens.shape)
    )
    small_grad = jnp.concatenate(
        [
            piece.astype(jnp.bfloat16).reshape(shards, -1)
            for piece in (
                first_gain_grad,
                second_gain_grad,
                bias_grad[:query_width],
                bias_grad[query_width : query_width + key_width],
                bias_grad[query_width + key_width :],
            )
        ],
        axis=1,
    )
    extra_rows = small.shape[0]
    small_grad = jnp.pad(
        small_grad, ((0, 0), (0, extra_rows * qkv_width - small_grad.shape[1]))
    ).reshape(shards, extra_rows, qkv_width)
    first_owned = lax.psum_scatter(
        jnp.concatenate([qkv_grad.reshape(shards, own_rows, qkv_width), small_grad], axis=1),
        "shard",
        scatter_dimension=0,
        tiled=False,
    )
    first_owned = rep_sum(first_owned, reps)
    out_owned = rep_sum(later_owned[:, :model_width], reps)
    hidden_set = rep_ordered(later_owned[:, model_width:], reps, rep_index)
    down_set = rep_ordered(down_owned, reps, rep_index).reshape(own_hidden, model_width)

    def spread_columns(parts):
        grouped = parts.reshape(reps, own_rows, shards, part_hidden)
        return grouped.transpose(1, 2, 0, 3).reshape(own_rows, hidden_width).astype(jnp.float32)

    small_owned = first_owned[own_rows:].reshape(-1)
    small_outs = [small_owned[starts[i] : starts[i] + sizes[i]] for i in range(len(sizes))]
    return (
        output,
        tokens_grad,
        small_outs[0],
        first_owned[:own_rows, :query_width],
        small_outs[2],
        first_owned[:own_rows, query_width : query_width + key_width],
        small_outs[3],
        first_owned[:own_rows, query_width + key_width :],
        small_outs[4],
        out_owned.astype(jnp.float32),
        small_outs[1],
        spread_columns(hidden_set[:, :, :slice_width]),
        spread_columns(hidden_set[:, :, padded_width:]),
        down_set.astype(jnp.float32),
    )


def solution(mesh):
    placed = (
        P("rep", "shard", None),
        P("rep", "shard"),
        P("shard"),
        P("shard", None),
        P("shard"),
        P("shard", None),
        P("shard"),
        P("shard", None),
        P("shard"),
        P("shard", None),
        P("shard"),
        P("shard", None),
        P("shard", None),
        P("shard", None),
        P("rep", "shard", None),
    )
    return jax.shard_map(
        functools.partial(on_device, reps=mesh.shape["rep"], shards=mesh.shape["shard"]),
        mesh=mesh,
        in_specs=placed,
        out_specs=(
            P("rep", "shard", None),
            P("rep", "shard", None),
            P("shard"),
            P("shard", None),
            P("shard"),
            P("shard", None),
            P("shard"),
            P("shard", None),
            P("shard"),
            P("shard", None),
            P("shard"),
            P("shard", None),
            P("shard", None),
            P("shard", None),
        ),
        check_vma=False,
    )
```
